32 devices in a mesh: groups: 2 (over x), ctx: 16 (over z, y, core).
Axes of the slice: x: 2, y: 2, z: 4, core: 2. Of those that a mesh axis runs over, the one named last changes fastest.
Arguments:
- activations: bfloat16 [2, 4096, 8192], P('groups', 'ctx'), parts along dimension 0, may hold values from -6 to 6
- in_projection: bfloat16 [2, 64, 8192], replicated, may hold values from -0.0625 to 0.0625
- out_projection: bfloat16 [2, 64, 1024], replicated, may hold values from -0.1875 to 0.1875
- out_grads: bfloat16 [2, 2, 4096, 1024], P(None, 'groups', 'ctx'), parts along dimension 1, may hold values from -6 to 6
- gram: float32 [2, 8192, 4096], P(None, ('groups', 'ctx')), parts along dimension 1, may hold values from -6 to 6
Outputs:
- gram_new: float32 [2, 8192, 4096], P(None, ('groups', 'ctx')), parts along dimension 1
The draws below stay inside these ranges and needn't reach their ends.
There are 2 independent parts, one for each index of `groups`. The reference program is written for one: setup_inputs(seed, part) draws one part's arguments, and reference() takes and returns one part's arrays. A program takes and returns all parts, laid end to end along the dimension named above; an argument that names none is the same for every part. Nothing has to cross between parts.
All inputs are finite; a program needn't handle non-finite values.
Results may differ from the reference program's by a relative error of at most 0.0003.
Values sent between devices are 32-bit elements; how exact they have to be, the bound alone decides.
A program may use at most 64 MiB of HBM per device.

```python
import math
import jax
import jax.numpy as jnp
from jax import lax

D = 8192
KV = 1024
K = 64
LAYERS = 2
DOCS = 1
SEQ = 4096
FEAT = 4096


def levels(stream_key, shape, pieces, low, largest):
    level, own = 1.0, jax.random.fold_in(stream_key, 6)
    for position, shards_of in pieces:
        draws = jnp.exp(jax.random.uniform(jax.random.fold_in(own, position), (shards_of,), jnp.float32, low / len(pieces), largest / len(pieces)))
        level = level * jnp.repeat(draws, shape[position] // shards_of).reshape([-1 if axis == position else 1 for axis in range(len(shape))])
    return level


def gaussian(key, dims, deviation, most, pieces=(), held_as=jnp.bfloat16):
    entries = jax.random.normal(key, dims, jnp.float32) * deviation
    if len(pieces) > 0:
        entries = levels(key, dims, pieces, -0.22, 0.18) * entries
    return jnp.clip(entries, min=-most, max=most).astype(held_as)


def setup_inputs(seed: int = 0, part: int = 0) -> dict:
    key_list = jax.random.split(jax.random.key(seed), 6)
    own_keys = jax.random.split(jax.random.fold_in(key_list[5], part), 6)
    return {
        "activations": gaussian(own_keys[0], (DOCS, SEQ, D), 1.0, 6.0, ((1, 16),)),
        "in_projection": gaussian(key_list[1], (LAYERS, K, D), D ** -0.5, 0.0625),
        "out_projection": gaussian(key_list[2], (LAYERS, K, KV), KV ** -0.5, 0.1875),
        "out_grads": gaussian(own_keys[3], (LAYERS, DOCS, SEQ, KV), 1.0, 6.0, ((2, 16),)),
        "gram": gaussian(own_keys[4], (LAYERS, FEAT, FEAT), 1.0, 6.0, ((1, 16),), jnp.float32),
    }


def reference(activations, in_projection, out_projection, out_grads, gram):
    flat = activations.reshape(DOCS * SEQ, D)
    stacked = in_projection.reshape(LAYERS * K, D)
    input_side = jnp.dot(flat, stacked.T, preferred_element_type=jnp.float32).reshape(DOCS, SEQ, LAYERS, K)
    grad_side = jnp.einsum('ldtv,lkv->ldtk', out_grads.astype(jnp.float32), out_projection.astype(jnp.float32), precision=lax.Precision.HIGHEST)
    features = jnp.einsum('ldta,dtlb->ldab', grad_side, input_side, precision=lax.Precision.HIGHEST)
    features = features.reshape(LAYERS, DOCS, FEAT) * (1.0 / math.sqrt(SEQ))
    update = jnp.einsum('ldr,ldc->lrc', features, features, precision=lax.Precision.HIGHEST)
    return gram + update
```

```python
import functools
import math

import jax
import jax.numpy as jnp
from jax import lax
from jax.experimental import pallas as pl
from jax.experimental.pallas import tpu as pltpu
from jax.sharding import PartitionSpec as P

MESH = pl.DeviceIdType.MESH
NT = (((1,), (1,)), ((), ()))


def exchange(
    n, norm, chunks, acts, inp, outp, grads, gram,
    rows_out, col_out, gram_out,
    acts_v, inp_v, outp_v, grads_v, parts, recv, own_v, every,
    load_sem, gram_sem, send1, recv1, send2, recv2,
):
    me = lax.axis_index("ctx")
    layers, rank = outp.shape[0], outp.shape[1]
    per = rank // n
    width = acts.shape[2]
    step = width // chunks

    def peer(d):
        return lax.rem(me + d, n)

    small = [
        pltpu.make_async_copy(outp, outp_v, load_sem.at[2 * chunks]),
        pltpu.make_async_copy(grads, grads_v, load_sem.at[2 * chunks + 1]),
    ]
    loads = []
    for k in range(chunks):
        cols = pl.ds(k * step, step)
        loads.append((
            pltpu.make_async_copy(acts.at[0, :, cols], acts_v.at[k], load_sem.at[2 * k]),
            pltpu.make_async_copy(inp.at[:, cols], inp_v.at[k], load_sem.at[2 * k + 1]),
        ))
    for copy in small:
        copy.start()
    for pair in loads:
        for copy in pair:
            copy.start()

    barrier = pltpu.get_barrier_semaphore()

    @pl.loop(1, n)
    def _(d):
        pl.semaphore_signal(barrier, inc=1, device_id={"ctx": peer(d)}, device_id_type=MESH)

    for copy in small:
        copy.wait()
    sides = [
        lax.dot_general(outp_v[l], grads_v[l, 0], NT, preferred_element_type=jnp.float32)
        for l in range(layers)
    ]
    x = None
    for k in range(chunks):
        for copy in loads[k]:
            copy.wait()
        term = lax.dot_general(acts_v[k], inp_v[k], NT, preferred_element_type=jnp.float32)
        x = term if x is None else x + term
    gram_copy = pltpu.make_async_copy(gram, gram_out, gram_sem)
    gram_copy.start()

    lane = lax.broadcasted_iota(jnp.int32, (rank, layers * rank), 1)
    part = None
    for l in range(layers):
        term = jnp.dot(
            sides[l], x, precision=lax.Precision.HIGHEST, preferred_element_type=jnp.float32
        )
        part = term if part is None else jnp.where(lane >= l * rank, term, part)
    for j in range(n):
        parts[j] = part[j * per:(j + 1) * per]

    pl.semaphore_wait(barrier, n - 1)

    def first(d):
        return pltpu.make_async_remote_copy(
            src_ref=parts.at[peer(d)], dst_ref=recv.at[d],
            send_sem=send1.at[d], recv_sem=recv1.at[d],
            device_id={"ctx": peer(d)}, device_id_type=MESH,
        )

    @pl.loop(1, n)
    def _(d):
        first(d).start()

    recv[0] = parts[me]

    @pl.loop(1, n)
    def _(d):
        first(d).wait_recv()

    total = jnp.sum(recv[...], axis=0) * norm
    for a in range(per):
        for l in range(layers):
            own_v[l:l + 1, a * rank:(a + 1) * rank] = total[a:a + 1, l * rank:(l + 1) * rank]

    def second(d):
        return pltpu.make_async_remote_copy(
            src_ref=own_v, dst_ref=every.at[me],
            send_sem=send2.at[d], recv_sem=recv2.at[d],
            device_id={"ctx": peer(d)}, device_id_type=MESH,
        )

    @pl.loop(1, n)
    def _(d):
        second(d).start()

    own = own_v[...]
    every[me] = own
    padded = jnp.concatenate([own] * (8 // layers), axis=0)
    col_out[...] = padded.T

    @pl.loop(1, n)
    def _(d):
        pltpu.make_async_remote_copy(
            src_ref=own_v, dst_ref=every.at[lax.rem(me + n - d, n)],
            send_sem=send2.at[d], recv_sem=recv2.at[d],
            device_id={"ctx": peer(d)}, device_id_type=MESH,
        ).wait_recv()

    wide = per * rank
    for j in range(n):
        rows_out[:, j * wide:(j + 1) * wide] = every[j]

    @pl.loop(1, n)
    def _(d):
        first(d).wait_send()
        second(d).wait_send()

    gram_copy.wait()


def update(block, rows, col, gram, out, out_v, sems):
    layers, height = gram.shape[0], gram.shape[1]
    copies = []
    for l in range(layers):
        row = rows[l:l + 1, :]
        for k in range(height // block):
            @pl.loop(0, block // 8)
            def _(i):
                at = pl.ds(pl.multiple_of(k * block + i * 8, 8), 8)
                out_v[l, at, :] = gram[l, at, :] + col[at, l:l + 1] * row

            at = pl.ds(k * block, block)
            copy = pltpu.make_async_copy(
                out_v.at[l, at], out.at[l, at], sems.at[l, k]
            )
            copy.start()
            copies.append(copy)
    for copy in copies:
        copy.wait()


def shards(activations, in_projection, out_projection, out_grads, gram):
    n = lax.axis_size("ctx")
    tokens, width = activations.shape[1], activations.shape[2]
    layers, rank = in_projection.shape[0], in_projection.shape[1]
    feat = rank * rank
    local = feat // n
    norm = 1.0 / math.sqrt(tokens * n)
    chunks = 4
    step = width // chunks
    flat = in_projection.reshape(layers * rank, width)
    anywhere = pl.BlockSpec(memory_space=pl.ANY)
    vmem = pl.BlockSpec(memory_space=pltpu.VMEM)
    f32, bf16 = jnp.float32, jnp.bfloat16
    dma = pltpu.SemaphoreType.DMA
    rows, col, held = pl.pallas_call(
        functools.partial(exchange, n, norm, chunks),
        out_shape=(
            jax.ShapeDtypeStruct((layers, feat), f32),
            jax.ShapeDtypeStruct((local, 8), f32),
            pltpu.VMEM(gram.shape, f32),
        ),
        in_specs=[anywhere] * 5,
        out_specs=(vmem, vmem, vmem),
        scratch_shapes=[
            pltpu.VMEM((chunks, tokens, step), bf16),
            pltpu.VMEM((chunks, layers * rank, step), bf16),
            pltpu.VMEM(out_projection.shape, bf16),
            pltpu.VMEM(out_grads.shape, bf16),
            pltpu.VMEM((n, rank // n, layers * rank), f32),
            pltpu.VMEM((n, rank // n, layers * rank), f32),
            pltpu.VMEM((layers, local), f32),
            pltpu.VMEM((n, layers, local), f32),
            dma((2 * chunks + 2,)),
            dma,
            dma((n,)), dma((n,)), dma((n,)), dma((n,)),
        ],
        compiler_params=pltpu.CompilerParams(
            collective_id=0, has_side_effects=True, vmem_limit_bytes=40 << 20
        ),
        name="exchange",
    )(activations, flat, out_projection, out_grads, gram)
    block = 32 if local % 32 == 0 else 8
    return pl.pallas_call(
        functools.partial(update, block),
        out_shape=jax.ShapeDtypeStruct(gram.shape, f32),
        in_specs=[vmem, vmem, vmem],
        out_specs=anywhere,
        scratch_shapes=[
            pltpu.VMEM(gram.shape, f32),
            dma((layers, local // block)),
        ],
        compiler_params=pltpu.CompilerParams(vmem_limit_bytes=32 << 20),
        name="update",
    )(rows, col, held)


def solution(mesh):
    placed = (
        P("groups", "ctx", None),
        P(),
        P(),
        P(None, "groups", "ctx", None),
        P(None, ("groups", "ctx"), None),
    )
    return jax.shard_map(
        shards,
        mesh=mesh,
        in_specs=placed,
        out_specs=P(None, ("groups", "ctx"), None),
        check_vma=False,
    )
```

```python
import functools
import math

import jax
import jax.numpy as jnp
from jax import lax
from jax.experimental import pallas as pl
from jax.experimental.pallas import tpu as pltpu
from jax.sharding import PartitionSpec as P

MESH = pl.DeviceIdType.MESH
NT = (((1,), (1,)), ((), ()))


def split(value):
    high = value.astype(jnp.bfloat16)
    return high, (value - high.astype(jnp.float32)).astype(jnp.bfloat16)


def exchange(
    n, norm, chunks, acts, inp, outp, grads, gram,
    rows_out, col_out, gram_out,
    acts_v, inp_v, outp_v, grads_v, parts, recv, own_v, every,
    load_sem, gram_sem, send1, recv1, send2, recv2,
):
    me = lax.axis_index("ctx")
    layers, rank = outp.shape[0], outp.shape[1]
    per = rank // n
    width = acts.shape[2]
    step = width // chunks

    def peer(d):
        return lax.rem(me + d, n)

    small = [
        pltpu.make_async_copy(outp, outp_v, load_sem.at[2 * chunks]),
        pltpu.make_async_copy(grads, grads_v, load_sem.at[2 * chunks + 1]),
    ]
    loads = []
    for k in range(chunks):
        cols = pl.ds(k * step, step)
        loads.append((
            pltpu.make_async_copy(acts.at[0, :, cols], acts_v.at[k], load_sem.at[2 * k]),
            pltpu.make_async_copy(inp.at[:, cols], inp_v.at[k], load_sem.at[2 * k + 1]),
        ))
    for copy in small:
        copy.start()
    for pair in loads:
        for copy in pair:
            copy.start()

    barrier = pltpu.get_barrier_semaphore()

    @pl.loop(1, n)
    def _(d):
        pl.semaphore_signal(barrier, inc=1, device_id={"ctx": peer(d)}, device_id_type=MESH)

    for copy in small:
        copy.wait()
    sides = [
        lax.dot_general(outp_v[l], grads_v[l, 0], NT, preferred_element_type=jnp.float32)
        for l in range(layers)
    ]
    g_hi, g_lo = split(jnp.concatenate(sides, axis=0))
    x = None
    for k in range(chunks):
        for copy in loads[k]:
            copy.wait()
        term = lax.dot_general(acts_v[k], inp_v[k], NT, preferred_element_type=jnp.float32)
        x = term if x is None else x + term
    x_hi, x_lo = split(x)
    left = jnp.concatenate([g_hi, g_hi, g_lo], axis=1)
    right = jnp.concatenate([x_hi, x_lo, x_hi], axis=0)
    full = jnp.dot(left, right, preferred_element_type=jnp.float32)
    lane = lax.broadcasted_iota(jnp.int32, (rank, layers * rank), 1)
    part = full[:rank]
    for l in range(1, layers):
        part = jnp.where(lane >= l * rank, full[l * rank:(l + 1) * rank], part)
    for j in range(n):
        parts[j] = part[j * per:(j + 1) * per]

    pl.semaphore_wait(barrier, n - 1)

    def first(d):
        return pltpu.make_async_remote_copy(
            src_ref=parts.at[peer(d)], dst_ref=recv.at[d],
            send_sem=send1.at[d], recv_sem=recv1.at[d],
            device_id={"ctx": peer(d)}, device_id_type=MESH,
        )

    @pl.loop(1, n, unroll=True)
    def _(d):
        first(d).start()

    gram_copies = []
    for l in range(layers):
        copy = pltpu.make_async_copy(gram.at[l], gram_out.at[l], gram_sem.at[l])
        copy.start()
        gram_copies.append(copy)

    recv[0] = parts[me]

    @pl.loop(1, n)
    def _(d):
        first(d).wait_recv()

    total = jnp.sum(recv[...], axis=0) * norm
    for a in range(per):
        for l in range(layers):
            own_v[l:l + 1, a * rank:(a + 1) * rank] = total[a:a + 1, l * rank:(l + 1) * rank]

    def second(d):
        return pltpu.make_async_remote_copy(
            src_ref=own_v, dst_ref=every.at[me],
            send_sem=send2.at[d], recv_sem=recv2.at[d],
            device_id={"ctx": peer(d)}, device_id_type=MESH,
        )

    @pl.loop(1, n, unroll=True)
    def _(d):
        second(d).start()

    own = own_v[...]
    every[me] = own
    padded = jnp.concatenate([own] * (8 // layers), axis=0)
    turned = padded.T
    for l in range(layers):
        col_out[l] = jnp.broadcast_to(turned[:, l:l + 1], col_out.shape[1:])

    @pl.loop(1, n)
    def _(d):
        pltpu.make_async_remote_copy(
            src_ref=own_v, dst_ref=every.at[lax.rem(me + n - d, n)],
            send_sem=send2.at[d], recv_sem=recv2.at[d],
            device_id={"ctx": peer(d)}, device_id_type=MESH,
        ).wait_recv()

    wide = per * rank
    for j in range(n):
        for l in range(layers):
            rows_out[l, :, j * wide:(j + 1) * wide] = jnp.broadcast_to(every[j, l:l + 1], (8, wide))

    @pl.loop(1, n)
    def _(d):
        first(d).wait_send()
        second(d).wait_send()

    for copy in gram_copies:
        copy.wait()


def update(block, rows, col, gram, out, out_v, sems):
    layers, height, feat = gram.shape
    lanes = col.shape[2]
    span = 8 * lanes
    for l in range(layers):
        @pl.loop(0, height // block)
        def _(k):
            base = pl.multiple_of(k * block, block)
            for c in range(0, feat, span):
                row = rows[l, :, c:c + span]
                for i in range(0, block, 8):
                    at = pl.ds(base + i, 8)
                    scale = jnp.concatenate([col[l, at, :]] * (span // lanes), axis=1)
                    out_v[l, at, c:c + span] = gram[l, at, c:c + span] + scale * row
            at = pl.ds(base, block)
            pltpu.make_async_copy(out_v.at[l, at], out.at[l, at], sems.at[l, k]).start()

    for l in range(layers):
        @pl.loop(0, height // block)
        def _(k):
            at = pl.ds(pl.multiple_of(k * block, block), block)
            pltpu.make_async_copy(out_v.at[l, at], out.at[l, at], sems.at[l, k]).wait()


def shards(activations, in_projection, out_projection, out_grads, gram):
    n = lax.axis_size("ctx")
    tokens, width = activations.shape[1], activations.shape[2]
    layers, rank = in_projection.shape[0], in_projection.shape[1]
    feat = rank * rank
    local = feat // n
    norm = 1.0 / math.sqrt(tokens * n)
    chunks = 8
    step = width // chunks
    flat = in_projection.reshape(layers * rank, width)
    hbm = pl.BlockSpec(memory_space=pltpu.HBM)
    vmem = pl.BlockSpec(memory_space=pltpu.VMEM)
    f32, bf16 = jnp.float32, jnp.bfloat16
    dma = pltpu.SemaphoreType.DMA
    rows, col, held = pl.pallas_call(
        functools.partial(exchange, n, norm, chunks),
        out_shape=(
            pltpu.VMEM((layers, 8, feat), f32),
            pltpu.VMEM((layers, local, 128), f32),
            pltpu.VMEM(gram.shape, f32),
        ),
        in_specs=[hbm] * 5,
        out_specs=(vmem, vmem, vmem),
        scratch_shapes=[
            pltpu.VMEM((chunks, tokens, step), bf16),
            pltpu.VMEM((chunks, layers * rank, step), bf16),
            pltpu.VMEM(out_projection.shape, bf16),
            pltpu.VMEM(out_grads.shape, bf16),
            pltpu.VMEM((n, rank // n, layers * rank), f32),
            pltpu.VMEM((n, rank // n, layers * rank), f32),
            pltpu.VMEM((layers, local), f32),
            pltpu.VMEM((n, layers, local), f32),
            dma((2 * chunks + 2,)),
            dma((layers,)),
            dma((n,)), dma((n,)), dma((n,)), dma((n,)),
        ],
        compiler_params=pltpu.CompilerParams(
            collective_id=0, has_side_effects=True, vmem_limit_bytes=40 << 20
        ),
        name="exchange",
    )(*(pltpu.with_memory_space_constraint(v, pltpu.HBM) for v in (activations, flat, out_projection, out_grads, gram)))
    block = 32 if local % 32 == 0 else 8
    return pl.pallas_call(
        functools.partial(update, block),
        out_shape=jax.ShapeDtypeStruct(gram.shape, f32),
        in_specs=[vmem, vmem, vmem],
        out_specs=hbm,
        scratch_shapes=[
            pltpu.VMEM(gram.shape, f32),
            dma((layers, local // block)),
        ],
        compiler_params=pltpu.CompilerParams(vmem_limit_bytes=32 << 20),
        name="update",
    )(rows, col, held)


def solution(mesh):
    placed = (
        P("groups", "ctx", None),
        P(),
        P(),
        P(None, "groups", "ctx", None),
        P(None, ("groups", "ctx"), None),
    )
    return jax.shard_map(
        shards,
        mesh=mesh,
        in_specs=placed,
        out_specs=P(None, ("groups", "ctx"), None),
        check_vma=False,
    )
```

```python
import functools
import math

import jax
import jax.numpy as jnp
from jax import lax
from jax.experimental import pallas as pl
from jax.experimental.pallas import tpu as pltpu
from jax.sharding import PartitionSpec as P

MESH = pl.DeviceIdType.MESH
NT = (((1,), (1,)), ((), ()))


def split(value):
    high = value.astype(jnp.bfloat16)
    return high, (value - high.astype(jnp.float32)).astype(jnp.bfloat16)


def exchange(
    n, norm, chunks, acts, inp, outp, grads, gram,
    rows_out, col_out, gram_out,
    acts_v, inp_v, outp_v, grads_v, parts, recv, own_v, every,
    load_sem, gram_sem, send1, recv1, send2, recv2,
):
    me = lax.axis_index("ctx")
    layers, rank = outp.shape[0], outp.shape[1]
    per = rank // n
    width = acts.shape[2]
    step = width // chunks

    def peer(d):
        return lax.rem(me + d, n)

    small = [
        pltpu.make_async_copy(outp, outp_v, load_sem.at[2 * chunks]),
        pltpu.make_async_copy(grads, grads_v, load_sem.at[2 * chunks + 1]),
    ]
    loads = []
    for k in range(chunks):
        cols = pl.ds(k * step, step)
        loads.append((
            pltpu.make_async_copy(acts.at[0, :, cols], acts_v.at[k], load_sem.at[2 * k]),
            pltpu.make_async_copy(inp.at[:, cols], inp_v.at[k], load_sem.at[2 * k + 1]),
        ))
    ahead = 3
    for pair in loads[:ahead] + [small]:
        for copy in pair:
            copy.start()

    barrier = pltpu.get_barrier_semaphore()

    @pl.loop(1, n)
    def _(d):
        pl.semaphore_signal(barrier, inc=1, device_id={"ctx": peer(d)}, device_id_type=MESH)

    x = None
    for k in range(chunks):
        for copy in loads[k]:
            copy.wait()
        if k + ahead < chunks:
            for copy in loads[k + ahead]:
                copy.start()
        if k == chunks - 2:
            for copy in small:
                copy.wait()
            sides = [
                lax.dot_general(outp_v[l], grads_v[l, 0], NT, preferred_element_type=jnp.float32)
                for l in range(layers)
            ]
            g_hi, g_lo = split(jnp.concatenate(sides, axis=0))
        term = lax.dot_general(acts_v[k], inp_v[k], NT, preferred_element_type=jnp.float32)
        x = term if x is None else x + term
    x_hi, x_lo = split(x)
    left = jnp.concatenate([g_hi, g_hi, g_lo], axis=1)
    right = jnp.concatenate([x_hi, x_lo, x_hi], axis=0)
    full = jnp.dot(left, right, preferred_element_type=jnp.float32)
    lane = lax.broadcasted_iota(jnp.int32, (rank, layers * rank), 1)
    part = full[:rank]
    for l in range(1, layers):
        part = jnp.where(lane >= l * rank, full[l * rank:(l + 1) * rank], part)
    for j in range(n):
        parts[j] = part[j * per:(j + 1) * per]

    pl.semaphore_wait(barrier, n - 1)

    def first(d):
        return pltpu.make_async_remote_copy(
            src_ref=parts.at[peer(d)], dst_ref=recv.at[d],
            send_sem=send1.at[d], recv_sem=recv1.at[d],
            device_id={"ctx": peer(d)}, device_id_type=MESH,
        )

    @pl.loop(1, n, unroll=True)
    def _(d):
        first(d).start()

    gram_copies = []
    for l in range(layers):
        copy = pltpu.make_async_copy(gram.at[l], gram_out.at[l], gram_sem.at[l])
        copy.start()
        gram_copies.append(copy)

    recv[0] = parts[me]

    @pl.loop(1, n)
    def _(d):
        first(d).wait_recv()

    total = jnp.sum(recv[...], axis=0) * norm
    for a in range(per):
        for l in range(layers):
            own_v[l:l + 1, a * rank:(a + 1) * rank] = total[a:a + 1, l * rank:(l + 1) * rank]

    def second(d):
        return pltpu.make_async_remote_copy(
            src_ref=own_v, dst_ref=every.at[me],
            send_sem=send2.at[d], recv_sem=recv2.at[d],
            device_id={"ctx": peer(d)}, device_id_type=MESH,
        )

    @pl.loop(1, n, unroll=True)
    def _(d):
        second(d).start()

    own = own_v[...]
    padded = jnp.concatenate([own] * (8 // layers), axis=0)
    turned = padded.T
    for l in range(layers):
        col_out[l] = jnp.broadcast_to(turned[:, l:l + 1], col_out.shape[1:])

    @pl.loop(1, n)
    def _(d):
        first(d).wait_send()

    for copy in gram_copies:
        copy.wait()

    @pl.loop(1, n)
    def _(d):
        second(d).wait_send()

    for l in range(layers):
        rows_out[l, me] = jnp.broadcast_to(own[l:l + 1], (8, own.shape[1]))

    @pl.loop(1, n, unroll=True)
    def _(d):
        source = lax.rem(me + n - d, n)
        pltpu.make_async_remote_copy(
            src_ref=own_v, dst_ref=every.at[source],
            send_sem=send2.at[d], recv_sem=recv2.at[d],
            device_id={"ctx": peer(d)}, device_id_type=MESH,
        ).wait_recv()
        block = every[source]
        for l in range(layers):
            rows_out[l, source] = jnp.broadcast_to(block[l:l + 1], (8, block.shape[1]))


def update(block, rows, col, gram, out, out_v, sems):
    layers, height, feat = gram.shape
    lanes = col.shape[2]
    span = rows.shape[3]
    piece = min(span, lanes)
    for l in range(layers):
        @pl.loop(0, height // block)
        def _(k):
            base = pl.multiple_of(k * block, block)
            for j in range(feat // span):
                row = rows[l, j]
                c = j * span
                for i in range(0, block, 8):
                    at = pl.ds(base + i, 8)
                    scale = jnp.concatenate([col[l, at, :piece]] * (span // piece), axis=1)
                    out_v[l, at, c:c + span] = gram[l, at, c:c + span] + scale * row
            at = pl.ds(base, block)
            pltpu.make_async_copy(out_v.at[l, at], out.at[l, at], sems.at[l, k]).start()

    for l in range(layers):
        @pl.loop(0, height // block)
        def _(k):
            at = pl.ds(pl.multiple_of(k * block, block), block)
            pltpu.make_async_copy(out_v.at[l, at], out.at[l, at], sems.at[l, k]).wait()


def shards(activations, in_projection, out_projection, out_grads, gram):
    n = lax.axis_size("ctx")
    tokens, width = activations.shape[1], activations.shape[2]
    layers, rank = in_projection.shape[0], in_projection.shape[1]
    feat = rank * rank
    local = feat // n
    norm = 1.0 / math.sqrt(tokens * n)
    chunks = 4
    step = width // chunks
    flat = in_projection.reshape(layers * rank, width)
    hbm = pl.BlockSpec(memory_space=pltpu.HBM)
    vmem = pl.BlockSpec(memory_space=pltpu.VMEM)
    f32, bf16 = jnp.float32, jnp.bfloat16
    dma = pltpu.SemaphoreType.DMA
    rows, col, held = pl.pallas_call(
        functools.partial(exchange, n, norm, chunks),
        out_shape=(
            pltpu.VMEM((layers, n, 8, local), f32),
            pltpu.VMEM((layers, local, 128), f32),
            pltpu.VMEM(gram.shape, f32),
        ),
        in_specs=[hbm] * 5,
        out_specs=(vmem, vmem, vmem),
        scratch_shapes=[
            pltpu.VMEM((chunks, tokens, step), bf16),
            pltpu.VMEM((chunks, layers * rank, step), bf16),
            pltpu.VMEM(out_projection.shape, bf16),
            pltpu.VMEM(out_grads.shape, bf16),
            pltpu.VMEM((n, rank // n, layers * rank), f32),
            pltpu.VMEM((n, rank // n, layers * rank), f32),
            pltpu.VMEM((layers, local), f32),
            pltpu.VMEM((n, layers, local), f32),
            dma((2 * chunks + 2,)),
            dma((layers,)),
            dma((n,)), dma((n,)), dma((n,)), dma((n,)),
        ],
        compiler_params=pltpu.CompilerParams(
            collective_id=0, has_side_effects=True, vmem_limit_bytes=40 << 20
        ),
        name="exchange",
    )(*(pltpu.with_memory_space_constraint(v, pltpu.HBM) for v in (activations, flat, out_projection, out_grads, gram)))
    block = 32 if local % 32 == 0 else 8
    return pl.pallas_call(
        functools.partial(update, block),
        out_shape=jax.ShapeDtypeStruct(gram.shape, f32),
        in_specs=[vmem, vmem, vmem],
        out_specs=hbm,
        scratch_shapes=[
            pltpu.VMEM(gram.shape, f32),
            dma((layers, local // block)),
        ],
        compiler_params=pltpu.CompilerParams(vmem_limit_bytes=32 << 20),
        name="update",
    )(rows, col, held)


def solution(mesh):
    placed = (
        P("groups", "ctx", None),
        P(),
        P(),
        P(None, "groups", "ctx", None),
        P(None, ("groups", "ctx"), None),
    )
    return jax.shard_map(
        shards,
        mesh=mesh,
        in_specs=placed,
        out_specs=P(None, ("groups", "ctx"), None),
        check_vma=False,
    )
```

```python
import functools
import math

import jax
import jax.numpy as jnp
from jax import lax
from jax.experimental import pallas as pl
from jax.experimental.pallas import tpu as pltpu
from jax.sharding import PartitionSpec as P

MESH = pl.DeviceIdType.MESH
NT = (((1,), (1,)), ((), ()))


def split(value):
    high = value.astype(jnp.bfloat16)
    return high, (value - high.astype(jnp.float32)).astype(jnp.bfloat16)


def exchange(
    n, norm, chunks, acts, inp, outp, grads, gram,
    rows_out, col_out, gram_out,
    acts_v, inp_v, outp_v, grads_v, parts, recv, own_v, every,
    load_sem, gram_sem, send1, recv1, send2, recv2,
):
    me = lax.axis_index("ctx")
    layers, rank = outp.shape[0], outp.shape[1]
    per = rank // n
    width = acts.shape[2]
    step = width // chunks

    def peer(d):
        return lax.rem(me + d, n)

    small = [
        pltpu.make_async_copy(outp, outp_v, load_sem.at[2 * chunks]),
        pltpu.make_async_copy(grads, grads_v, load_sem.at[2 * chunks + 1]),
    ]
    loads = []
    for k in range(chunks):
        cols = pl.ds(k * step, step)
        loads.append((
            pltpu.make_async_copy(acts.at[0, :, cols], acts_v.at[k], load_sem.at[2 * k]),
            pltpu.make_async_copy(inp.at[:, cols], inp_v.at[k], load_sem.at[2 * k + 1]),
        ))
    ahead = 3
    for pair in loads[:ahead] + [small]:
        for copy in pair:
            copy.start()

    barrier = pltpu.get_barrier_semaphore()

    @pl.loop(1, n)
    def _(d):
        pl.semaphore_signal(barrier, inc=1, device_id={"ctx": peer(d)}, device_id_type=MESH)

    x = None
    for k in range(chunks):
        for copy in loads[k]:
            copy.wait()
        if k + ahead < chunks:
            for copy in loads[k + ahead]:
                copy.start()
        if k == chunks - 2:
            for copy in small:
                copy.wait()
            sides = [
                lax.dot_general(outp_v[l], grads_v[l, 0], NT, preferred_element_type=jnp.float32)
                for l in range(layers)
            ]
            g_hi, g_lo = split(jnp.concatenate(sides, axis=0))
        term = lax.dot_general(acts_v[k], inp_v[k], NT, preferred_element_type=jnp.float32)
        x = term if x is None else x + term
    x_hi, x_lo = split(x)
    left = jnp.concatenate([g_hi, g_hi, g_lo], axis=1)
    right = jnp.concatenate([x_hi, x_lo, x_hi], axis=0)
    full = jnp.dot(left, right, preferred_element_type=jnp.float32)
    lane = lax.broadcasted_iota(jnp.int32, (rank, layers * rank), 1)
    part = full[:rank]
    for l in range(1, layers):
        part = jnp.where(lane >= l * rank, full[l * rank:(l + 1) * rank], part)
    for j in range(n):
        parts[j] = part[j * per:(j + 1) * per]

    pl.semaphore_wait(barrier, n - 1)

    def first(d):
        return pltpu.make_async_remote_copy(
            src_ref=parts.at[peer(d)], dst_ref=recv.at[d],
            send_sem=send1.at[d], recv_sem=recv1,
            device_id={"ctx": peer(d)}, device_id_type=MESH,
        )

    @pl.loop(1, n, unroll=True)
    def _(d):
        first(d).start()

    gram_copies = []
    for l in range(layers):
        copy = pltpu.make_async_copy(gram.at[l], gram_out.at[l], gram_sem.at[l])
        copy.start()
        gram_copies.append(copy)

    recv[0] = parts[me]

    arrived = recv.at[pl.ds(1, n - 1)]
    pltpu.make_async_copy(arrived, arrived, recv1).wait()

    total = jnp.sum(recv[...], axis=0) * norm
    for a in range(per):
        for l in range(layers):
            own_v[l:l + 1, a * rank:(a + 1) * rank] = total[a:a + 1, l * rank:(l + 1) * rank]

    def second(d):
        return pltpu.make_async_remote_copy(
            src_ref=own_v, dst_ref=every.at[me],
            send_sem=send2.at[d], recv_sem=recv2.at[d],
            device_id={"ctx": peer(d)}, device_id_type=MESH,
        )

    @pl.loop(1, n, unroll=True)
    def _(d):
        second(d).start()

    own = own_v[...]
    padded = jnp.concatenate([own] * (8 // layers), axis=0)
    turned = padded.T
    for l in range(layers):
        col_out[l] = jnp.broadcast_to(turned[:, l:l + 1], col_out.shape[1:])

    @pl.loop(1, n)
    def _(d):
        first(d).wait_send()

    for copy in gram_copies:
        copy.wait()

    @pl.loop(1, n)
    def _(d):
        second(d).wait_send()

    for l in range(layers):
        rows_out[l, me] = jnp.broadcast_to(own[l:l + 1], (8, own.shape[1]))

    @pl.loop(1, n, unroll=True)
    def _(d):
        source = lax.rem(me + n - d, n)
        pltpu.make_async_remote_copy(
            src_ref=own_v, dst_ref=every.at[source],
            send_sem=send2.at[d], recv_sem=recv2.at[d],
            device_id={"ctx": peer(d)}, device_id_type=MESH,
        ).wait_recv()
        block = every[source]
        for l in range(layers):
            rows_out[l, source] = jnp.broadcast_to(block[l:l + 1], (8, block.shape[1]))


def update(block, rows, col, gram, out, out_v, sems):
    layers, height, feat = gram.shape
    lanes = col.shape[2]
    span = rows.shape[3]
    piece = min(span, lanes)
    for l in range(layers):
        @pl.loop(0, height // block)
        def _(k):
            base = pl.multiple_of(k * block, block)
            for j in range(feat // span):
                row = rows[l, j]
                c = j * span
                for i in range(0, block, 8):
                    at = pl.ds(base + i, 8)
                    scale = jnp.concatenate([col[l, at, :piece]] * (span // piece), axis=1)
                    out_v[l, at, c:c + span] = gram[l, at, c:c + span] + scale * row
            at = pl.ds(base, block)
            pltpu.make_async_copy(out_v.at[l, at], out.at[l, at], sems.at[l, k]).start()

    for l in range(layers):
        @pl.loop(0, height // block)
        def _(k):
            at = pl.ds(pl.multiple_of(k * block, block), block)
            pltpu.make_async_copy(out_v.at[l, at], out.at[l, at], sems.at[l, k]).wait()


def shards(activations, in_projection, out_projection, out_grads, gram):
    n = lax.axis_size("ctx")
    tokens, width = activations.shape[1], activations.shape[2]
    layers, rank = in_projection.shape[0], in_projection.shape[1]
    feat = rank * rank
    local = feat // n
    norm = 1.0 / math.sqrt(tokens * n)
    chunks = 4
    step = width // chunks
    flat = in_projection.reshape(layers * rank, width)
    hbm = pl.BlockSpec(memory_space=pltpu.HBM)
    vmem = pl.BlockSpec(memory_space=pltpu.VMEM)
    f32, bf16 = jnp.float32, jnp.bfloat16
    dma = pltpu.SemaphoreType.DMA
    rows, col, held = pl.pallas_call(
        functools.partial(exchange, n, norm, chunks),
        out_shape=(
            pltpu.VMEM((layers, n, 8, local), f32),
            pltpu.VMEM((layers, local, 128), f32),
            pltpu.VMEM(gram.shape, f32),
        ),
        in_specs=[hbm] * 5,
        out_specs=(vmem, vmem, vmem),
        scratch_shapes=[
            pltpu.VMEM((chunks, tokens, step), bf16),
            pltpu.VMEM((chunks, layers * rank, step), bf16),
            pltpu.VMEM(out_projection.shape, bf16),
            pltpu.VMEM(out_grads.shape, bf16),
            pltpu.VMEM((n, rank // n, layers * rank), f32),
            pltpu.VMEM((n, rank // n, layers * rank), f32),
            pltpu.VMEM((layers, local), f32),
            pltpu.VMEM((n, layers, local), f32),
            dma((2 * chunks + 2,)),
            dma((layers,)),
            dma((n,)), dma, dma((n,)), dma((n,)),
        ],
        compiler_params=pltpu.CompilerParams(
            collective_id=0, has_side_effects=True, vmem_limit_bytes=40 << 20
        ),
        name="exchange",
    )(*(pltpu.with_memory_space_constraint(v, pltpu.HBM) for v in (activations, flat, out_projection, out_grads, gram)))
    block = 32 if local % 32 == 0 else 8
    return pl.pallas_call(
        functools.partial(update, block),
        out_shape=jax.ShapeDtypeStruct(gram.shape, f32),
        in_specs=[vmem, vmem, vmem],
        out_specs=hbm,
        scratch_shapes=[
            pltpu.VMEM(gram.shape, f32),
            dma((layers, local // block)),
        ],
        compiler_params=pltpu.CompilerParams(vmem_limit_bytes=32 << 20),
        name="update",
    )(rows, col, held)


def solution(mesh):
    placed = (
        P("groups", "ctx", None),
        P(),
        P(),
        P(None, "groups", "ctx", None),
        P(None, ("groups", "ctx"), None),
    )
    return jax.shard_map(
        shards,
        mesh=mesh,
        in_specs=placed,
        out_specs=P(None, ("groups", "ctx"), None),
        check_vma=False,
    )
```
